32 devices in a mesh: ens: 2 (over y), lon: 4 (over z), lat: 4 (over x, core).
Axes of the slice: x: 2, y: 2, z: 4, core: 2. Of those that a mesh axis runs over, the one named last changes fastest.
Arguments:
- tracers: float32 [2, 16, 768, 512], P(None, 'ens', 'lat', 'lon'), parts along dimension 1, may hold values from -6 to 6
- velocities: float32 [2, 16, 768, 512], P(None, 'ens', 'lat', 'lon'), parts along dimension 1, may hold values from -0.6 to 0.6
- land_mask: int32 [768, 512], P('lat', 'lon'), may hold values 0 or 1
- atm_flux: float32 [768, 512], P(('ens', 'lat'), 'lon'), parts along dimension 0, may hold values from -6 to 6
- atm_id: int32 [48, 4], P('lat'), may hold values from 0 to 23, as said below
- intersection_count: int32 [48], P('lat'), may hold values from 1 to 4, as said below
- weight_tiles: float32 [48, 4, 16, 16], P('lat'), may hold values from 0 to 0.25
Outputs:
- new_tracers: float32 [2, 16, 768, 512], P(None, 'ens', 'lat', 'lon'), parts along dimension 1
- ocean_flux: float32 [1536, 512], P(('ens', 'lat'), 'lon'), parts along dimension 0
The draws below stay inside these ranges and needn't reach their ends.
There are 2 independent parts, one for each index of `ens`. The reference program is written for one: setup_inputs(seed, part) draws one part's arguments, and reference() takes and returns one part's arrays. A program takes and returns all parts, laid end to end along the dimension named above; an argument that names none is the same for every part. Nothing has to cross between parts.
Inputs may be any that keep to these rules, and one draw needn't show every extreme that they name: `atm_id`: entry k of ocean block b names an atmosphere block within b // 2 - 2 to b // 2 + 2; a block's entries are consecutive blocks, the last used one repeated past its count; both ends of that reach occur. `intersection_count`: entries of a block at or past its count are ignored.
All inputs are finite; a program needn't handle non-finite values. No bound on the sum of `land_mask` on one device may be relied on, other than what follows from the above.
Results may differ from the reference program's by a relative error of at most 0.000078.
Values sent between devices are 32-bit elements; how exact they have to be, the bound alone decides.
A program may use at most 64 MiB of HBM per device.

```python
import jax
import jax.numpy as jnp
from jax import lax

LEV = 8
RB = 16
KMAX = 4
ITERS = 2
NLON = 512
NLAT = 768
NATM = 384
OCEAN_BLOCKS = 48
ATM_BLOCKS = 24


def intersection_lists(key):
    key_count, key_start = jax.random.split(key)
    ocean_index = jnp.arange(OCEAN_BLOCKS, dtype=jnp.int32)
    counts = jax.random.randint(key_count, (OCEAN_BLOCKS,), 1, KMAX + 1, dtype=jnp.int32)
    counts = jnp.where(ocean_index % 4 == 1, KMAX, counts)
    lowest = ocean_index // 2 - 2
    highest = ocean_index // 2 + 2 - (counts - 1)
    random_bits = jax.random.randint(key_start, (OCEAN_BLOCKS,), 0, 1 << 20, dtype=jnp.int32)
    starts = lowest + random_bits % (highest - lowest + 1)
    starts = jnp.where(ocean_index % 4 == 0, lowest, starts)
    starts = jnp.where(ocean_index % 4 == 3, highest, starts)
    offsets = jnp.minimum(jnp.arange(KMAX, dtype=jnp.int32)[None, :], counts[:, None] - 1)
    intersection_ids = jnp.clip(starts[:, None] + offsets, 0, ATM_BLOCKS - 1)
    return (intersection_ids, counts)


def draw_atm_id(key, part):
    return intersection_lists(key)[0]


def draw_intersection_count(key, part):
    return intersection_lists(key)[1]


def set_ends(values, rng, low, largest):
    place = [jax.random.randint(jax.random.fold_in(rng, axis), (), 0, length) for axis, length in enumerate(values.shape)]
    widest = values.shape.index(max(values.shape))
    beside = place[:widest] + [(place[widest] + 1) % values.shape[widest]] + place[widest + 1:]
    return values.at[tuple(place)].set(low).at[tuple(beside)].set(largest)


def steps_of(key, shape, cuts, smallest, top_value):
    level, own = 1.0, jax.random.fold_in(key, 6)
    for axis_at, parts in cuts:
        draws = jnp.exp(jax.random.uniform(jax.random.fold_in(own, axis_at), (parts,), jnp.float32, smallest / len(cuts), top_value / len(cuts)))
        level = level * jnp.repeat(draws, shape[axis_at] // parts).reshape([-1 if axis == axis_at else 1 for axis in range(len(shape))])
    return level


def centred(stream_key, extent, spread, most, cuts=(), held_as=jnp.bfloat16):
    values = jax.random.normal(stream_key, extent, jnp.float32) * spread
    if len(cuts) > 0:
        values = steps_of(stream_key, extent, cuts, -0.22, 0.18) * values
    return jnp.clip(values, min=-most, max=most).astype(held_as)


def setup_inputs(seed: int = 0, part: int = 0) -> dict:
    splits = jax.random.split(jax.random.key(seed), 8)
    part_keys = jax.random.split(jax.random.fold_in(splits[7], part), 8)
    tracers = centred(part_keys[0], (2, LEV, NLAT, NLON), 1.0, 6.0, ((2, 4), (3, 4)), jnp.float32)
    velocities = centred(part_keys[1], (2, LEV, NLAT, NLON), 0.15, 0.6, ((2, 4), (3, 4)), jnp.float32)
    land_mask = set_ends((jax.random.randint(splits[2], (NLAT, NLON), 0, 8) < 7).astype(jnp.int32), jax.random.fold_in(splits[2], 1), 0, 1)
    atm_flux = centred(part_keys[3], (NATM, NLON), 1.0, 6.0, ((0, 4), (1, 4)), jnp.float32)
    atm_id = draw_atm_id(jax.random.fold_in(splits[7], 71), part)
    intersection_count = draw_intersection_count(jax.random.fold_in(splits[7], 71), part)
    weight_tiles = jnp.clip(0.25 * jax.random.uniform(splits[6], (OCEAN_BLOCKS, KMAX, RB, RB), jnp.float32) ** steps_of(splits[6], (OCEAN_BLOCKS, KMAX, RB, RB), ((0, 4),), -0.2, 0.2), 0.0, 0.25)
    return {"tracers": tracers, "velocities": velocities, "land_mask": land_mask, "atm_flux": atm_flux, "atm_id": atm_id, "intersection_count": intersection_count, "weight_tiles": weight_tiles}


lateral_mix = 0.06
biharmonic_mix = 0.015
vertical_mix = 0.15
heat_gain = 0.5


def laplacian(values, open_east, open_north):
    grad_east = open_east * (values[..., 1:] - values[..., :-1])
    grad_north = open_north * (values[..., 1:, :] - values[..., :-1, :])
    return (grad_east[..., 1:-1, 1:] - grad_east[..., 1:-1, :-1]) + (grad_north[..., 1:, 1:-1] - grad_north[..., :-1, 1:-1])


def advance_field(field, east_vel, north_vel, ocean_mask, surface, gain):
    open_east = ocean_mask[:, :-1] * ocean_mask[:, 1:]
    open_north = ocean_mask[:-1, :] * ocean_mask[1:, :]
    diff_east = field[..., 1:] - field[..., :-1]
    diff_north = field[..., 1:, :] - field[..., :-1, :]
    vel_east = 0.5 * (east_vel[..., 1:] + east_vel[..., :-1])
    vel_north = 0.5 * (north_vel[..., 1:, :] + north_vel[..., :-1, :])
    flux_east = open_east * (vel_east * 0.5 * (field[..., 1:] + field[..., :-1]) - lateral_mix * diff_east)
    flux_north = open_north * (vel_north * 0.5 * (field[..., 1:, :] + field[..., :-1, :]) - lateral_mix * diff_north)
    advection = -(flux_east[..., 1:-1, 1:] - flux_east[..., 1:-1, :-1]) - (flux_north[..., 1:, 1:-1] - flux_north[..., :-1, 1:-1])
    first_lap = laplacian(field, open_east, open_north)
    second_lap = laplacian(first_lap, open_east[1:-1, 1:-1], open_north[1:-1, 1:-1])
    centre = field[..., 2:-2, 2:-2]
    diff_down = centre[1:] - centre[:-1]
    top_zero = jnp.zeros_like(centre[:1])
    vertical = vertical_mix * (jnp.concatenate([diff_down, top_zero], 0) - jnp.concatenate([top_zero, diff_down], 0))
    heating = jnp.concatenate([(gain * heat_gain) * surface[2:-2, 2:-2][None], jnp.zeros_like(centre[1:])], 0)
    change = advection[..., 1:-1, 1:-1] - biharmonic_mix * second_lap + vertical + heating
    return centre + ocean_mask[2:-2, 2:-2] * change


def extend_field(field, margin_cells, fold_signs):
    south_rows = jnp.zeros((field.shape[0], margin_cells, field.shape[2]), jnp.float32)
    north_rows = field[:, field.shape[1] - margin_cells:, :][:, ::-1, ::-1] * fold_signs[:, None, None]
    widened = jnp.concatenate([south_rows, field, north_rows], 1)
    return jnp.concatenate([widened[..., -margin_cells:], widened, widened[..., :margin_cells]], 2)


def reference(tracers, velocities, land_mask, atm_flux, atm_id, intersection_count, weight_tiles):
    blocks_atm = atm_flux.reshape(ATM_BLOCKS, RB, NLON)
    picked = blocks_atm[atm_id]
    in_use = (jnp.arange(KMAX, dtype=jnp.int32)[None, :] < intersection_count[:, None]).astype(jnp.float32)
    weights_used = weight_tiles * in_use[:, :, None, None]
    ocean_flux = jnp.einsum("bkrs,bksc->brc", weights_used, picked, precision=lax.Precision.HIGHEST).reshape(NLAT, NLON)
    ocean_mask = land_mask.astype(jnp.float32)
    statics = jnp.concatenate([velocities.reshape(2 * LEV, NLAT, NLON), ocean_mask[None], ocean_flux[None]], 0)
    static_signs = jnp.concatenate([-jnp.ones((2 * LEV,), jnp.float32), jnp.ones((2,), jnp.float32)])
    static_ext = extend_field(statics, 2, static_signs)
    east_vel = static_ext[:LEV]
    north_vel = static_ext[LEV:2 * LEV]
    mask_ext = static_ext[2 * LEV]
    surface = static_ext[2 * LEV + 1]
    gains = jnp.array([1.0, 0.0], jnp.float32)
    tracer_signs = jnp.ones((2 * LEV,), jnp.float32)
    state = tracers
    for iteration in range(ITERS):
        extended = extend_field(state.reshape(2 * LEV, NLAT, NLON), 2, tracer_signs).reshape(2, LEV, NLAT + 4, NLON + 4)
        state = lax.map(lambda member: advance_field(member[0], east_vel, north_vel, mask_ext, surface, member[1]), (extended, gains))
    return state, ocean_flux
```

```python
import functools

import jax
import jax.numpy as jnp
from jax import lax
from jax.experimental import pallas as pl
from jax.experimental.pallas import tpu as pltpu
from jax.sharding import PartitionSpec as P

lateral_mix = 0.06
biharmonic_mix = 0.015
vertical_mix = 0.15
heat_gain = 0.5

LANES = 128
BASE = 16
CHUNK = 16
MESH = pl.DeviceIdType.MESH
V, MASK, U = 0, 3, 4


def roll(x, shift):
    return pltpu.roll(x, shift % LANES if isinstance(shift, int) else shift, x.ndim - 1)


def kernel(
    lat_n, lon_n, levels, rows, blocks, entries, block_rows, local_atm,
    tr, vel, mask_in, atm, wt, ids, cnt, out, flux_out,
    F, G, MI, HE, HN, OE, ON, PL, A, R2, FE, FL, ATM, WT, WB,
    SNS, RNS, RC, SEW, REW,
    in_sem, out_sem, send_sem, recv_sem, atm_sem,
):
    end = BASE + rows
    tiles = rows // 8
    third = tiles // 8
    fold_rows = third * 8
    lat, lon = lax.axis_index("lat"), lax.axis_index("lon")
    top = lat == lat_n - 1
    bottom = lat == 0
    west = lax.rem(lon + lon_n - 1, lon_n)
    east = lax.rem(lon + 1, lon_n)
    up_lat = jnp.where(top, lat, lat + 1)
    up_lon = jnp.where(top, lon_n - 1 - lon, lon)
    a_lon = jnp.where(top, lax.rem(lon_n - lon, lon_n), east)
    b_lon = jnp.where(top, lax.rem(2 * lon_n - 2 - lon, lon_n), west)
    a_self = jnp.logical_and(top, a_lon == lon)
    b_self = jnp.logical_and(top, b_lon == lon)
    a_away = jnp.logical_not(a_self)
    b_away = jnp.logical_not(b_self)
    inner = jnp.logical_not(bottom)
    below = jnp.maximum(lat - 1, 0)
    up_slot = jnp.where(top, 0, 1)
    a_slot = jnp.where(top, 0, 2)
    b_slot = jnp.where(top, 1, 3)

    lane = lax.broadcasted_iota(jnp.int32, (8, LANES), 1)
    lane_c = lax.broadcasted_iota(jnp.int32, (CHUNK, LANES), 1)
    j8 = lane % 16
    jc = lane_c % 16

    loads = [
        pltpu.make_async_copy(vel.at[1], F.at[V, 0:levels, BASE:end], in_sem.at[0]),
        pltpu.make_async_copy(tr.at[0], F.at[1, 0:levels, BASE:end], in_sem.at[1]),
        pltpu.make_async_copy(tr.at[1], F.at[2, 0:levels, BASE:end], in_sem.at[2]),
        pltpu.make_async_copy(mask_in, MI, in_sem.at[3]),
        pltpu.make_async_copy(vel.at[0], F.at[U, 0:levels, BASE:end], in_sem.at[4]),
        pltpu.make_async_copy(atm, ATM.at[2 * block_rows : 2 * block_rows + local_atm * block_rows], in_sem.at[5]),
        pltpu.make_async_copy(wt, WT, in_sem.at[6]),
    ]
    for copy in (loads[5], loads[3], loads[1], loads[2], loads[4], loads[0], loads[6]):
        copy.start()

    barrier = pltpu.get_barrier_semaphore()

    def greet(lat_to, lon_to):
        pl.semaphore_signal(barrier, inc=1, device_id={"lat": lat_to, "lon": lon_to}, device_id_type=MESH)

    greet(lat, west)
    greet(lat, east)
    greet(up_lat, up_lon)
    pl.when(a_away)(lambda: greet(up_lat, a_lon))
    pl.when(b_away)(lambda: greet(up_lat, b_lon))

    @pl.when(inner)
    def _():
        greet(below, lon)
        greet(below, west)
        greet(below, east)

    zero8 = jnp.zeros((8, LANES), jnp.float32)

    def zero_slot(s, carry):
        for side in (0, 1):
            SNS[side, s, 16:24] = zero8
        return carry

    lax.fori_loop(0, 7, zero_slot, 0)

    @pl.when(bottom)
    def _():
        def clear(s, carry):
            for tile in range(3):
                RNS[1, s, 8 * tile : 8 * tile + 8] = zero8
            RC[2, s] = zero8
            RC[3, s] = zero8
            return carry

        lax.fori_loop(0, 7, clear, 0)
        for tile in range(2 * block_rows // 8):
            ATM[8 * tile : 8 * tile + 8] = zero8

    atm_end = (2 + local_atm) * block_rows

    @pl.when(top)
    def _():
        for tile in range(2 * block_rows // 8):
            ATM[atm_end + 8 * tile : atm_end + 8 * tile + 8] = zero8

    def remote(src, dst, send, recv, lat_to, lon_to):
        return pltpu.make_async_remote_copy(
            src_ref=src, dst_ref=dst, send_sem=send, recv_sem=recv,
            device_id={"lat": lat_to, "lon": lon_to}, device_id_type=MESH,
        )

    def messages(ph, n0, n1, e0, e1):
        s, r = send_sem, recv_sem
        edge = lambda side: SNS.at[side, n0:n1, 16:24]
        return {
            "up": remote(SNS.at[0, n0:n1], RNS.at[up_slot, n0:n1], s.at[ph, 0], r.at[ph, up_slot], up_lat, up_lon),
            "a": remote(edge(0), RC.at[a_slot, n0:n1], s.at[ph, 2], r.at[ph, 2 + a_slot], up_lat, a_lon),
            "b": remote(edge(0), RC.at[b_slot, n0:n1], s.at[ph, 3], r.at[ph, 2 + b_slot], up_lat, b_lon),
            "down": remote(SNS.at[1, n0:n1], RNS.at[0, n0:n1], s.at[ph, 1], r.at[ph, 0], below, lon),
            "se": remote(edge(1), RC.at[0, n0:n1], s.at[ph, 4], r.at[ph, 2], below, east),
            "sw": remote(edge(1), RC.at[1, n0:n1], s.at[ph, 5], r.at[ph, 3], below, west),
            "w": remote(SEW.at[0, e0:e1], REW.at[1, e0:e1], s.at[ph, 6], r.at[ph, 7], lat, west),
            "e": remote(SEW.at[1, e0:e1], REW.at[0, e0:e1], s.at[ph, 7], r.at[ph, 6], lat, east),
        }

    def arrivals(ph, n0, n1, e0, e1):
        s, r = send_sem, recv_sem
        edge = SNS.at[0, n0:n1, 16:24]
        got = {}
        for slot in (0, 1):
            got[slot] = remote(SNS.at[0, n0:n1], RNS.at[slot, n0:n1], s.at[ph, 0], r.at[ph, slot], lat, west)
        for slot in range(4):
            got[2 + slot] = remote(edge, RC.at[slot, n0:n1], s.at[ph, 2], r.at[ph, 2 + slot], lat, west)
        for slot in (0, 1):
            got[6 + slot] = remote(SEW.at[0, e0:e1], REW.at[slot, e0:e1], s.at[ph, 6], r.at[ph, 6 + slot], lat, west)
        return got

    def send_ew(ph, n0, n1, e0, e1):
        m = messages(ph, n0, n1, e0, e1)
        m["w"].start()
        m["e"].start()

    def send_ns(ph, n0, n1, e0, e1):
        m = messages(ph, n0, n1, e0, e1)

        @pl.when(inner)
        def _():
            m["down"].start()
            m["se"].start()
            m["sw"].start()

        @pl.when(top)
        def _():
            r_i = lax.broadcasted_iota(jnp.int32, (LANES, LANES), 0)
            c_i = lax.broadcasted_iota(jnp.int32, (LANES, LANES), 1)
            whole = jnp.where(r_i + c_i == LANES - 1, 1.0, 0.0).astype(jnp.float32)
            group = jnp.where((r_i // 16 == c_i // 16) & (r_i % 16 + c_i % 16 == 15), 1.0, 0.0).astype(jnp.float32)
            for f in range(n0, n1):
                sign = -1.0 if f == V else 1.0
                body = SNS[0, f, 0:16]
                tail = SNS[0, f, 16:24]
                SNS[0, f, 0:16] = sign * jnp.dot(
                    body, whole, precision=lax.Precision.HIGHEST, preferred_element_type=jnp.float32
                )
                SNS[0, f, 16:24] = sign * jnp.dot(
                    tail, group, precision=lax.Precision.HIGHEST, preferred_element_type=jnp.float32
                )

        m["up"].start()
        pl.when(a_away)(m["a"].start)
        pl.when(b_away)(m["b"].start)

        @pl.when(a_self)
        def _():
            for f in range(n0, n1):
                RC[0, f] = SNS[0, f, 16:24]

        @pl.when(b_self)
        def _():
            for f in range(n0, n1):
                RC[1, f] = SNS[0, f, 16:24]

    def wait_all(ph, n0, n1, e0, e1):
        got = arrivals(ph, n0, n1, e0, e1)
        got[0].wait_recv()
        pl.when(a_away)(got[2].wait_recv)
        pl.when(b_away)(got[3].wait_recv)
        got[6].wait_recv()
        got[7].wait_recv()

        @pl.when(inner)
        def _():
            got[1].wait_recv()
            got[4].wait_recv()
            got[5].wait_recv()

    def wait_sent(ph, n0, n1, e0, e1):
        m = messages(ph, n0, n1, e0, e1)
        m["up"].wait_send()
        m["w"].wait_send()
        m["e"].wait_send()
        pl.when(a_away)(m["a"].wait_send)
        pl.when(b_away)(m["b"].wait_send)

        @pl.when(inner)
        def _():
            m["down"].wait_send()
            m["se"].wait_send()
            m["sw"].wait_send()

    def finish_pack(B, s, gather):
        to_w = [zero8] * third
        to_e = [zero8] * third
        for i in range(tiles):
            a = gather(i)
            own = jnp.where(j8 < 8, roll(a, -4), roll(a, 4))
            B[levels, BASE + 8 * i : BASE + 8 * i + 8] = own
            p, r = i // third, i % third
            here = j8 // 2 == p
            to_w[r] = jnp.where(here, roll(own, 2 * p - 4), to_w[r])
            to_e[r] = jnp.where(here, roll(own, 2 * p - 10), to_e[r])
        for r in range(third):
            SEW[0, s, 8 * r : 8 * r + 8] = to_w[r]
            SEW[1, s, 8 * r : 8 * r + 8] = to_e[r]

    def pack_rows(B, s):
        for side, first, second in ((0, end - 1, end - 2), (1, BASE, BASE + 1)):
            for l in range(levels):
                SNS[side, s, l : l + 1] = B[l, first : first + 1]
                SNS[side, s, levels + l : levels + l + 1] = B[l, second : second + 1]
            SNS[side, s, 16:17] = B[levels, first : first + 1]
            SNS[side, s, 17:18] = B[levels, second : second + 1]

    def gather_planes(B):
        def gather(i):
            a = zero8
            for l in range(levels):
                a = jnp.where(lane // 16 == l, roll(B[l, BASE + 8 * i : BASE + 8 * i + 8], 16 * l + 8), a)
            return a

        return gather

    def unpack_rows(B, s):
        for l in range(levels):
            B[l, end : end + 1] = RNS[0, s, l : l + 1]
            B[l, end + 1 : end + 2] = RNS[0, s, levels + l : levels + l + 1]
            B[l, BASE - 1 : BASE] = RNS[1, s, l : l + 1]
            B[l, BASE - 2 : BASE - 1] = RNS[1, s, levels + l : levels + l + 1]
        for side, first, second in ((0, end, end + 1), (1, BASE - 1, BASE - 2)):
            own = RNS[side, s, 16:24]
            w = roll(RC[2 * side, s], -8)
            e = roll(RC[2 * side + 1, s], 8)
            x = jnp.where(j8 < 4, w, jnp.where(j8 >= 12, e, own))
            B[levels, first : first + 1] = x[0:1]
            B[levels, second : second + 1] = x[1:2]

    def unpack_cols(B, s):
        for i in range(tiles):
            p, r = i // third, i % third
            at = slice(BASE + 8 * i, BASE + 8 * i + 8)
            w = roll(REW[0, s, 8 * r : 8 * r + 8], 2 - 2 * p)
            e = roll(REW[1, s, 8 * r : 8 * r + 8], 12 - 2 * p)
            B[levels, at] = jnp.where(j8 < 4, w, jnp.where(j8 >= 12, e, B[levels, at]))

    pl.semaphore_wait(
        barrier, 3 + jnp.where(a_away, 1, 0) + jnp.where(b_away, 1, 0) + jnp.where(inner, 3, 0)
    )
    reach = 2 * block_rows
    loads[5].wait()
    atm_up = remote(ATM.at[atm_end - reach : atm_end], ATM.at[0:reach], atm_sem.at[0], atm_sem.at[2], up_lat, up_lon)
    atm_down = remote(
        ATM.at[reach : 2 * reach], ATM.at[atm_end : atm_end + reach], atm_sem.at[1], atm_sem.at[3], below, lon
    )
    pl.when(jnp.logical_not(top))(atm_up.start)
    pl.when(inner)(atm_down.start)

    loads[3].wait()

    def spread_mask(l, carry):
        F[MASK, l, BASE:end] = MI[...].astype(jnp.float32)
        return carry

    lax.fori_loop(0, levels, spread_mask, 0)
    for index in (1, 2, 4, 0):
        loads[index].wait()

    def pack_field(f, carry):
        B = F.at[f]
        finish_pack(B, f, gather_planes(B))
        pack_rows(B, f)
        return carry

    lax.fori_loop(0, 5, pack_field, 0)
    first = (0, 0, 4, 1, 5)
    send_ew(*first)
    send_ns(*first)

    loads[6].wait()
    slots = local_atm + 4
    wide = slots * block_rows
    spread = jnp.where(
        lax.broadcasted_iota(jnp.int32, (block_rows, wide), 1) % block_rows
        == lax.broadcasted_iota(jnp.int32, (block_rows, wide), 0),
        1.0, 0.0,
    ).astype(jnp.float32)
    slot_of = lax.broadcasted_iota(jnp.int32, (block_rows, wide), 1) // block_rows

    def build(b, carry):
        flat = jnp.concatenate([WT[b, k] for k in range(entries)], 0)
        copies = jnp.dot(flat, spread, precision=lax.Precision.HIGHEST, preferred_element_type=jnp.float32)
        total = jnp.zeros((block_rows, wide), jnp.float32)
        for k in range(entries):
            slot = jnp.where(k < cnt[b], ids[b, k] - lat * local_atm + 2, -1)
            total = total + jnp.where(slot_of == slot, copies[k * block_rows : (k + 1) * block_rows], 0.0)
        WB[pl.ds(pl.multiple_of(b * block_rows, block_rows), block_rows)] = total
        return carry

    lax.fori_loop(0, blocks, build, 0)
    pl.when(inner)(
        remote(ATM.at[0:reach], ATM.at[0:reach], atm_sem.at[0], atm_sem.at[2], lat, west).wait_recv
    )
    pl.when(jnp.logical_not(top))(
        remote(ATM.at[0:reach], ATM.at[atm_end : atm_end + reach], atm_sem.at[1], atm_sem.at[3], lat, west).wait_recv
    )
    FL[...] = jnp.dot(WB[...], ATM[...], precision=lax.Precision.HIGHEST, preferred_element_type=jnp.float32)
    flux_copy = pltpu.make_async_copy(FL, flux_out, in_sem.at[7])
    flux_copy.start()
    for i in range(tiles):
        at = slice(8 * i, 8 * i + 8)
        a = roll(FL[at], 8)
        own = jnp.where(j8 < 8, roll(a, -4), roll(a, 4))
        FE[at] = jnp.where(lane < 16, heat_gain * own, 0.0)

    wait_all(*first)

    def place_rows(f, carry):
        unpack_rows(F.at[f], f)
        return carry

    def place_cols(f, carry):
        unpack_cols(F.at[f], f)
        return carry

    lax.fori_loop(0, 4, place_rows, 0)
    lax.fori_loop(1, 5, place_cols, 0)

    for kind, plane in ((0, 0), (1, levels)):
        for r in range(8, end + 8, 8):
            m = F[MASK, plane, r : r + 8]
            OE[kind, r : r + 8] = m * roll(m, -1)
            ON[kind, r : r + 8] = m * F[MASK, plane, r + 1 : r + 9]

    def face_tables(l, carry):
        kind = jnp.where(l == levels, 1, 0)
        for r in range(8, end, 8):
            at = slice(r, r + 8)
            HN[l, at] = 0.25 * ON[kind, at] * (F[V, l, at] + F[V, l, r + 1 : r + 9])
            if r >= BASE:
                u = F[U, l, at]
                HE[l, at] = 0.25 * OE[kind, at] * (u + roll(u, -1))
        return carry

    lax.fori_loop(0, levels + 1, face_tables, 0)

    def first_pass(B, l, kind):
        for r in range(8, end + 8, CHUNK):
            at = slice(r, r + CHUNK)
            q = B[l, at]
            ge = OE[kind, at] * (roll(q, -1) - q)
            lap = (ge - roll(ge, 1)) + (
                ON[kind, at] * (B[l, r + 1 : r + 1 + CHUNK] - q)
                - ON[kind, r - 1 : r - 1 + CHUNK] * (q - B[l, r - 1 : r - 1 + CHUNK])
            )
            PL[at] = biharmonic_mix * lap - lateral_mix * q

    def second_pass(B, l, kind, r, vertical, heat):
        at, up, dn = slice(r, r + CHUNK), slice(r + 1, r + 1 + CHUNK), slice(r - 1, r - 1 + CHUNK)
        q, qn, qs = B[l, at], B[l, up], B[l, dn]
        p, pn, ps = PL[at], PL[up], PL[dn]
        te = HE[l, at] * (q + roll(q, -1)) + OE[kind, at] * (roll(p, -1) - p)
        tn = HN[l, at] * (q + qn) + ON[kind, at] * (pn - p)
        ts = HN[l, dn] * (q + qs) + ON[kind, dn] * (p - ps)
        low, high = vertical(q, at)
        change = vertical_mix * ((low - q) + (high - q)) - ((te - roll(te, 1)) + (tn - ts))
        if heat is not None:
            change = change + heat
        return q + F[MASK, levels if kind == 1 else 0, at] * change

    def advance(B, C, t, packing):
        first_pass(B, levels, 1)
        for r in range(BASE, end, CHUNK):
            own = slice(r - BASE, r - BASE + CHUNK)

            def beside(q, at):
                return (
                    jnp.where(lane_c < 16, q, roll(q, 16)),
                    jnp.where(lane_c >= LANES - 16, q, roll(q, -16)),
                )

            res = second_pass(B, levels, 1, r, beside, FE[own] if t == 0 else None)
            R2[own] = jnp.where(jc < 2, roll(res, -10), roll(res, -2))

        def level(l, carry):
            first_pass(B, l, 0)
            back = lax.rem(2 * LANES - 2 - 16 * l, LANES)
            ahead = lax.rem(16 * l + 8, LANES)
            lower, upper = jnp.maximum(l - 1, 0), jnp.minimum(l + 1, levels - 1)
            gain = jnp.where(l == 0, heat_gain, 0.0).astype(jnp.float32)
            for r in range(BASE, end, CHUNK):
                own = slice(r - BASE, r - BASE + CHUNK)
                res = second_pass(
                    B, l, 0, r, lambda q, at: (B[lower, at], B[upper, at]), gain * FL[own] if t == 0 else None
                )
                res = jnp.where((lane_c < 2) | (lane_c >= LANES - 2), roll(R2[own], back), res)
                C[l, r : r + CHUNK] = res
                if packing:
                    A[own] = jnp.where(lane_c // 16 == l, roll(res, ahead), A[own])
            if not packing:
                pltpu.make_async_copy(C.at[l, BASE:end], out.at[t, l], out_sem.at[t, l]).start()
            return carry

        lax.fori_loop(0, levels, level, 0)

    later = ((1, 5, 6, 5, 6), (2, 6, 7, 6, 7))
    for t in (0, 1):
        advance(F.at[1 + t], G.at[t], t, True)
        finish_pack(G.at[t], 5 + t, lambda i: A[8 * i : 8 * i + 8])
        send_ew(*later[t])
        pack_rows(G.at[t], 5 + t)
        send_ns(*later[t])
    for t in (0, 1):
        wait_all(*later[t])
        unpack_rows(G.at[t], 5 + t)
        unpack_cols(G.at[t], 5 + t)
        advance(G.at[t], F.at[1 + t], t, False)

    pl.when(jnp.logical_not(top))(atm_up.wait_send)
    pl.when(inner)(atm_down.wait_send)
    wait_sent(*first)
    for t in (0, 1):
        wait_sent(*later[t])
    flux_copy.wait()

    def finish(l, carry):
        for t in (0, 1):
            pltpu.make_async_copy(F.at[1 + t, l, BASE:end], out.at[t, l], out_sem.at[t, l]).wait()
        return carry

    lax.fori_loop(0, levels, finish, 0)


def solution(mesh):
    lat_n, lon_n = mesh.shape["lat"], mesh.shape["lon"]

    def per_device(tracers, velocities, land_mask, atm_flux, atm_id, intersection_count, weight_tiles):
        _, levels, rows, cols = tracers.shape
        blocks, entries, block_rows, _ = weight_tiles.shape
        local_atm = atm_flux.shape[0] // block_rows
        planes = levels + 1
        tall = rows + 2 * BASE
        fold_rows = rows // 8
        f32 = jnp.float32
        hbm = pl.BlockSpec(memory_space=pl.ANY)
        smem = pl.BlockSpec(memory_space=pltpu.SMEM)
        return pl.pallas_call(
            functools.partial(kernel, lat_n, lon_n, levels, rows, blocks, entries, block_rows, local_atm),
            out_shape=(
                jax.ShapeDtypeStruct(tracers.shape, f32),
                jax.ShapeDtypeStruct((rows, cols), f32),
            ),
            in_specs=[hbm, hbm, hbm, hbm, hbm, smem, smem],
            out_specs=(hbm, hbm),
            scratch_shapes=[
                pltpu.VMEM((5, planes, tall, cols), f32),
                pltpu.VMEM((2, planes, tall, cols), f32),
                pltpu.VMEM((rows, cols), jnp.int32),
                pltpu.VMEM((planes, tall, cols), f32),
                pltpu.VMEM((planes, tall, cols), f32),
                pltpu.VMEM((2, tall, cols), f32),
                pltpu.VMEM((2, tall, cols), f32),
                pltpu.VMEM((tall, cols), f32),
                pltpu.VMEM((rows, cols), f32),
                pltpu.VMEM((rows, cols), f32),
                pltpu.VMEM((rows, cols), f32),
                pltpu.VMEM((rows, cols), f32),
                pltpu.VMEM(((local_atm + 4) * block_rows, cols), f32),
                pltpu.VMEM(weight_tiles.shape, f32),
                pltpu.VMEM((rows, (local_atm + 4) * block_rows), f32),
                pltpu.VMEM((2, 7, 24, cols), f32),
                pltpu.VMEM((2, 7, 24, cols), f32),
                pltpu.VMEM((4, 7, 8, cols), f32),
                pltpu.VMEM((2, 7, fold_rows, cols), f32),
                pltpu.VMEM((2, 7, fold_rows, cols), f32),
                pltpu.SemaphoreType.DMA((8,)),
                pltpu.SemaphoreType.DMA((2, levels)),
                pltpu.SemaphoreType.DMA((3, 8)),
                pltpu.SemaphoreType.DMA((3, 8)),
                pltpu.SemaphoreType.DMA((4,)),
            ],
            compiler_params=pltpu.CompilerParams(
                collective_id=0, has_side_effects=True, vmem_limit_bytes=40 * 1024 * 1024
            ),
        )(tracers, velocities, land_mask, atm_flux, weight_tiles, atm_id, intersection_count)

    in_specs = (
        P(None, "ens", "lat", "lon"),
        P(None, "ens", "lat", "lon"),
        P("lat", "lon"),
        P(("ens", "lat"), "lon"),
        P("lat", None),
        P("lat"),
        P("lat", None, None, None),
    )
    out_specs = (P(None, "ens", "lat", "lon"), P(("ens", "lat"), "lon"))
    return jax.shard_map(
        per_device, mesh=mesh, in_specs=in_specs, out_specs=out_specs, check_vma=False
    )
```

```python
import functools

import jax
import jax.numpy as jnp
from jax import lax
from jax.experimental import pallas as pl
from jax.experimental.pallas import tpu as pltpu
from jax.sharding import PartitionSpec as P

lateral_mix = 0.06
biharmonic_mix = 0.015
vertical_mix = 0.15
heat_gain = 0.5

LANES = 128
BASE = 16
CHUNK = 16
MESH = pl.DeviceIdType.MESH
V, MASK, U = 0, 3, 4


def roll(x, shift):
    return pltpu.roll(x, shift % LANES if isinstance(shift, int) else shift, x.ndim - 1)


def kernel(
    lat_n, lon_n, levels, rows, blocks, entries, block_rows, local_atm,
    tr, vel, mask_in, atm, wt, ids, cnt, out, flux_out,
    F, G, MI, HE, HN, OE, ON, PL, A, R2, FE, FL, ATM, WT, WB,
    SNS, RNS, RC, SEW, REW,
    in_sem, out_sem, send_sem, recv_sem, atm_sem,
):
    end = BASE + rows
    tiles = rows // 8
    third = tiles // 8
    fold_rows = third * 8
    lat, lon = lax.axis_index("lat"), lax.axis_index("lon")
    top = lat == lat_n - 1
    bottom = lat == 0
    west = lax.rem(lon + lon_n - 1, lon_n)
    east = lax.rem(lon + 1, lon_n)
    up_lat = jnp.where(top, lat, lat + 1)
    up_lon = jnp.where(top, lon_n - 1 - lon, lon)
    a_lon = jnp.where(top, lax.rem(lon_n - lon, lon_n), east)
    b_lon = jnp.where(top, lax.rem(2 * lon_n - 2 - lon, lon_n), west)
    a_self = jnp.logical_and(top, a_lon == lon)
    b_self = jnp.logical_and(top, b_lon == lon)
    a_away = jnp.logical_not(a_self)
    b_away = jnp.logical_not(b_self)
    inner = jnp.logical_not(bottom)
    below = jnp.maximum(lat - 1, 0)
    up_slot = jnp.where(top, 0, 1)
    a_slot = jnp.where(top, 0, 2)
    b_slot = jnp.where(top, 1, 3)

    lane = lax.broadcasted_iota(jnp.int32, (8, LANES), 1)
    lane_c = lax.broadcasted_iota(jnp.int32, (CHUNK, LANES), 1)
    j8 = lane & 15
    group8 = lane >> 4
    pair8 = j8 >> 1
    low8, high8, half8 = j8 < 4, j8 >= 12, j8 < 8
    group_c = lane_c >> 4
    jc_low = (lane_c & 15) < 2
    rim_c = (lane_c < 2) | (lane_c >= LANES - 2)
    first_c, last_c = lane_c < 16, lane_c >= LANES - 16

    loads = [
        pltpu.make_async_copy(vel.at[1], F.at[V, 0:levels, BASE:end], in_sem.at[0]),
        pltpu.make_async_copy(tr.at[0], F.at[1, 0:levels, BASE:end], in_sem.at[1]),
        pltpu.make_async_copy(tr.at[1], F.at[2, 0:levels, BASE:end], in_sem.at[2]),
        pltpu.make_async_copy(mask_in, MI, in_sem.at[3]),
        pltpu.make_async_copy(vel.at[0], F.at[U, 0:levels, BASE:end], in_sem.at[4]),
        pltpu.make_async_copy(atm, ATM.at[2 * block_rows : 2 * block_rows + local_atm * block_rows], in_sem.at[5]),
        pltpu.make_async_copy(wt, WT, in_sem.at[6]),
    ]
    for copy in (loads[5], loads[3], loads[1], loads[2], loads[4], loads[0], loads[6]):
        copy.start()

    barrier = pltpu.get_barrier_semaphore()

    def greet(lat_to, lon_to):
        pl.semaphore_signal(barrier, inc=1, device_id={"lat": lat_to, "lon": lon_to}, device_id_type=MESH)

    greet(lat, west)
    greet(lat, east)
    greet(up_lat, up_lon)
    pl.when(a_away)(lambda: greet(up_lat, a_lon))
    pl.when(b_away)(lambda: greet(up_lat, b_lon))

    @pl.when(inner)
    def _():
        greet(below, lon)
        greet(below, west)
        greet(below, east)

    zero8 = jnp.zeros((8, LANES), jnp.float32)

    def zero_slot(s, carry):
        for side in (0, 1):
            SNS[side, s, 16:24] = zero8
        return carry

    lax.fori_loop(0, 7, zero_slot, 0)

    @pl.when(bottom)
    def _():
        def clear(s, carry):
            for tile in range(3):
                RNS[1, s, 8 * tile : 8 * tile + 8] = zero8
            RC[2, s] = zero8
            RC[3, s] = zero8
            return carry

        lax.fori_loop(0, 7, clear, 0)
        for tile in range(2 * block_rows // 8):
            ATM[8 * tile : 8 * tile + 8] = zero8

    atm_end = (2 + local_atm) * block_rows

    @pl.when(top)
    def _():
        for tile in range(2 * block_rows // 8):
            ATM[atm_end + 8 * tile : atm_end + 8 * tile + 8] = zero8

    def remote(src, dst, send, recv, lat_to, lon_to):
        return pltpu.make_async_remote_copy(
            src_ref=src, dst_ref=dst, send_sem=send, recv_sem=recv,
            device_id={"lat": lat_to, "lon": lon_to}, device_id_type=MESH,
        )

    def messages(ph, n0, n1, e0, e1):
        s, r = send_sem, recv_sem
        edge = lambda side: SNS.at[side, n0:n1, 16:24]
        return {
            "up": remote(SNS.at[0, n0:n1], RNS.at[up_slot, n0:n1], s.at[ph, 0], r.at[ph, up_slot], up_lat, up_lon),
            "a": remote(edge(0), RC.at[a_slot, n0:n1], s.at[ph, 2], r.at[ph, 2 + a_slot], up_lat, a_lon),
            "b": remote(edge(0), RC.at[b_slot, n0:n1], s.at[ph, 3], r.at[ph, 2 + b_slot], up_lat, b_lon),
            "down": remote(SNS.at[1, n0:n1], RNS.at[0, n0:n1], s.at[ph, 1], r.at[ph, 0], below, lon),
            "se": remote(edge(1), RC.at[0, n0:n1], s.at[ph, 4], r.at[ph, 2], below, east),
            "sw": remote(edge(1), RC.at[1, n0:n1], s.at[ph, 5], r.at[ph, 3], below, west),
            "w": remote(SEW.at[0, e0:e1], REW.at[1, e0:e1], s.at[ph, 6], r.at[ph, 7], lat, west),
            "e": remote(SEW.at[1, e0:e1], REW.at[0, e0:e1], s.at[ph, 7], r.at[ph, 6], lat, east),
        }

    def arrivals(ph, n0, n1, e0, e1):
        s, r = send_sem, recv_sem
        edge = SNS.at[0, n0:n1, 16:24]
        got = {}
        for slot in (0, 1):
            got[slot] = remote(SNS.at[0, n0:n1], RNS.at[slot, n0:n1], s.at[ph, 0], r.at[ph, slot], lat, west)
        for slot in range(4):
            got[2 + slot] = remote(edge, RC.at[slot, n0:n1], s.at[ph, 2], r.at[ph, 2 + slot], lat, west)
        for slot in (0, 1):
            got[6 + slot] = remote(SEW.at[0, e0:e1], REW.at[slot, e0:e1], s.at[ph, 6], r.at[ph, 6 + slot], lat, west)
        return got

    def send_ew(ph, n0, n1, e0, e1):
        m = messages(ph, n0, n1, e0, e1)
        m["w"].start()
        m["e"].start()

    def send_ns(ph, n0, n1, e0, e1):
        m = messages(ph, n0, n1, e0, e1)

        @pl.when(inner)
        def _():
            m["down"].start()
            m["se"].start()
            m["sw"].start()

        @pl.when(top)
        def _():
            r_i = lax.broadcasted_iota(jnp.int32, (LANES, LANES), 0)
            c_i = lax.broadcasted_iota(jnp.int32, (LANES, LANES), 1)
            whole = jnp.where(r_i + c_i == LANES - 1, 1.0, 0.0).astype(jnp.float32)
            group = jnp.where((r_i // 16 == c_i // 16) & (r_i % 16 + c_i % 16 == 15), 1.0, 0.0).astype(jnp.float32)
            count = n1 - n0
            body = jnp.concatenate([SNS[0, f, 0:16] for f in range(n0, n1)], 0)
            tail = jnp.concatenate([SNS[0, f, 16:24] for f in range(n0, n1)], 0)
            body = jnp.dot(body, whole, precision=lax.Precision.HIGHEST, preferred_element_type=jnp.float32)
            tail = jnp.dot(tail, group, precision=lax.Precision.HIGHEST, preferred_element_type=jnp.float32)
            for i in range(count):
                sign = -1.0 if n0 + i == V else 1.0
                SNS[0, n0 + i, 0:16] = sign * body[16 * i : 16 * i + 16]
                SNS[0, n0 + i, 16:24] = sign * tail[8 * i : 8 * i + 8]

        m["up"].start()
        pl.when(a_away)(m["a"].start)
        pl.when(b_away)(m["b"].start)

        @pl.when(a_self)
        def _():
            for f in range(n0, n1):
                RC[0, f] = SNS[0, f, 16:24]

        @pl.when(b_self)
        def _():
            for f in range(n0, n1):
                RC[1, f] = SNS[0, f, 16:24]

    def wait_all(ph, n0, n1, e0, e1):
        got = arrivals(ph, n0, n1, e0, e1)
        got[0].wait_recv()
        pl.when(a_away)(got[2].wait_recv)
        pl.when(b_away)(got[3].wait_recv)
        got[6].wait_recv()
        got[7].wait_recv()

        @pl.when(inner)
        def _():
            got[1].wait_recv()
            got[4].wait_recv()
            got[5].wait_recv()

    def wait_sent(ph, n0, n1, e0, e1):
        m = messages(ph, n0, n1, e0, e1)
        m["up"].wait_send()
        m["w"].wait_send()
        m["e"].wait_send()
        pl.when(a_away)(m["a"].wait_send)
        pl.when(b_away)(m["b"].wait_send)

        @pl.when(inner)
        def _():
            m["down"].wait_send()
            m["se"].wait_send()
            m["sw"].wait_send()

    def finish_pack(B, s, gather):
        to_w = [zero8] * third
        to_e = [zero8] * third
        gathered = [gather(i) for i in range(tiles)]
        owns = [jnp.where(half8, roll(a, -4), roll(a, 4)) for a in gathered]
        for i, own in enumerate(owns):
            B[levels, BASE + 8 * i : BASE + 8 * i + 8] = own
            p, r = i // third, i % third
            here = pair8 == p
            to_w[r] = jnp.where(here, roll(own, 2 * p - 4), to_w[r])
            to_e[r] = jnp.where(here, roll(own, 2 * p - 10), to_e[r])
        for r in range(third):
            SEW[0, s, 8 * r : 8 * r + 8] = to_w[r]
            SEW[1, s, 8 * r : 8 * r + 8] = to_e[r]

    def pack_rows(B, s):
        for side, first, second in ((0, end - 1, end - 2), (1, BASE, BASE + 1)):
            for l in range(levels):
                SNS[side, s, l : l + 1] = B[l, first : first + 1]
                SNS[side, s, levels + l : levels + l + 1] = B[l, second : second + 1]
            SNS[side, s, 16:17] = B[levels, first : first + 1]
            SNS[side, s, 17:18] = B[levels, second : second + 1]

    def gather_planes(B):
        def gather(i):
            a = zero8
            for l in range(levels):
                a = jnp.where(group8 == l, roll(B[l, BASE + 8 * i : BASE + 8 * i + 8], 16 * l + 8), a)
            return a

        return gather

    def unpack_rows(B, s):
        for l in range(levels):
            B[l, end : end + 1] = RNS[0, s, l : l + 1]
            B[l, end + 1 : end + 2] = RNS[0, s, levels + l : levels + l + 1]
            B[l, BASE - 1 : BASE] = RNS[1, s, l : l + 1]
            B[l, BASE - 2 : BASE - 1] = RNS[1, s, levels + l : levels + l + 1]
        for side, first, second in ((0, end, end + 1), (1, BASE - 1, BASE - 2)):
            own = RNS[side, s, 16:24]
            w = roll(RC[2 * side, s], -8)
            e = roll(RC[2 * side + 1, s], 8)
            x = jnp.where(low8, w, jnp.where(high8, e, own))
            B[levels, first : first + 1] = x[0:1]
            B[levels, second : second + 1] = x[1:2]

    def unpack_cols(B, s):
        for i in range(tiles):
            p, r = i // third, i % third
            at = slice(BASE + 8 * i, BASE + 8 * i + 8)
            w = roll(REW[0, s, 8 * r : 8 * r + 8], 2 - 2 * p)
            e = roll(REW[1, s, 8 * r : 8 * r + 8], 12 - 2 * p)
            B[levels, at] = jnp.where(low8, w, jnp.where(high8, e, B[levels, at]))

    loads[3].wait()

    def spread_mask(l, carry):
        F[MASK, l, BASE:end] = MI[...].astype(jnp.float32)
        return carry

    lax.fori_loop(0, levels, spread_mask, 0)
    def pack_field(f, carry):
        B = F.at[f]
        finish_pack(B, f, gather_planes(B))
        pack_rows(B, f)
        return carry

    for f in (MASK, 1, 2, U, V):
        if f != MASK:
            loads[f].wait()
        pack_field(f, 0)

    pl.semaphore_wait(
        barrier, 3 + jnp.where(a_away, 1, 0) + jnp.where(b_away, 1, 0) + jnp.where(inner, 3, 0)
    )
    reach = 2 * block_rows
    loads[5].wait()
    atm_up = remote(ATM.at[atm_end - reach : atm_end], ATM.at[0:reach], atm_sem.at[0], atm_sem.at[2], up_lat, up_lon)
    atm_down = remote(
        ATM.at[reach : 2 * reach], ATM.at[atm_end : atm_end + reach], atm_sem.at[1], atm_sem.at[3], below, lon
    )
    pl.when(jnp.logical_not(top))(atm_up.start)
    pl.when(inner)(atm_down.start)

    first = (0, 0, 4, 1, 5)
    send_ew(*first)
    send_ns(*first)

    loads[6].wait()
    slots = local_atm + 4
    wide = slots * block_rows
    spread = jnp.where(
        lax.broadcasted_iota(jnp.int32, (block_rows, wide), 1) % block_rows
        == lax.broadcasted_iota(jnp.int32, (block_rows, wide), 0),
        1.0, 0.0,
    ).astype(jnp.float32)
    slot_of = lax.broadcasted_iota(jnp.int32, (block_rows, wide), 1) // block_rows

    def build(b, carry):
        flat = jnp.concatenate([WT[b, k] for k in range(entries)], 0)
        copies = jnp.dot(flat, spread, precision=lax.Precision.HIGHEST, preferred_element_type=jnp.float32)
        total = jnp.zeros((block_rows, wide), jnp.float32)
        for k in range(entries):
            slot = jnp.where(k < cnt[b], ids[k, b] - lat * local_atm + 2, -1)
            total = total + jnp.where(slot_of == slot, copies[k * block_rows : (k + 1) * block_rows], 0.0)
        WB[pl.ds(pl.multiple_of(b * block_rows, block_rows), block_rows)] = total
        return carry

    lax.fori_loop(0, blocks, build, 0)
    pl.when(inner)(
        remote(ATM.at[0:reach], ATM.at[0:reach], atm_sem.at[0], atm_sem.at[2], lat, west).wait_recv
    )
    pl.when(jnp.logical_not(top))(
        remote(ATM.at[0:reach], ATM.at[atm_end : atm_end + reach], atm_sem.at[1], atm_sem.at[3], lat, west).wait_recv
    )
    FL[...] = jnp.dot(WB[...], ATM[...], precision=lax.Precision.HIGHEST, preferred_element_type=jnp.float32)
    flux_copy = pltpu.make_async_copy(FL, flux_out, in_sem.at[7])
    flux_copy.start()
    for i in range(tiles):
        at = slice(8 * i, 8 * i + 8)
        a = roll(FL[at], 8)
        own = jnp.where(half8, roll(a, -4), roll(a, 4))
        FE[at] = jnp.where(lane < 16, heat_gain * own, 0.0)

    wait_all(*first)

    def place_rows(f, carry):
        unpack_rows(F.at[f], f)
        return carry

    def place_cols(f, carry):
        unpack_cols(F.at[f], f)
        return carry

    lax.fori_loop(0, 4, place_rows, 0)
    lax.fori_loop(1, 5, place_cols, 0)

    for kind, plane in ((0, 0), (1, levels)):
        for r in range(8, end + 8, 8):
            m = F[MASK, plane, r : r + 8]
            OE[kind, r : r + 8] = m * roll(m, -1)
            ON[kind, r : r + 8] = m * F[MASK, plane, r + 1 : r + 9]

    def face_tables(l, carry):
        kind = jnp.where(l == levels, 1, 0)
        for r in range(8, end, 8):
            at = slice(r, r + 8)
            HN[l, at] = 0.25 * ON[kind, at] * (F[V, l, at] + F[V, l, r + 1 : r + 9])
            if r >= BASE:
                u = F[U, l, at]
                HE[l, at] = 0.25 * OE[kind, at] * (u + roll(u, -1))
        return carry

    lax.fori_loop(0, levels + 1, face_tables, 0)

    def first_pass(B, l, kind):
        for r in range(8, end + 8, CHUNK):
            at = slice(r, r + CHUNK)
            q = B[l, at]
            ge = OE[kind, at] * (roll(q, -1) - q)
            lap = (ge - roll(ge, 1)) + (
                ON[kind, at] * (B[l, r + 1 : r + 1 + CHUNK] - q)
                - ON[kind, r - 1 : r - 1 + CHUNK] * (q - B[l, r - 1 : r - 1 + CHUNK])
            )
            PL[at] = biharmonic_mix * lap - lateral_mix * q

    def second_pass(B, l, kind, r, vertical, heat):
        at, up, dn = slice(r, r + CHUNK), slice(r + 1, r + 1 + CHUNK), slice(r - 1, r - 1 + CHUNK)
        q, qn, qs = B[l, at], B[l, up], B[l, dn]
        p, pn, ps = PL[at], PL[up], PL[dn]
        te = HE[l, at] * (q + roll(q, -1)) + OE[kind, at] * (roll(p, -1) - p)
        tn = HN[l, at] * (q + qn) + ON[kind, at] * (pn - p)
        ts = HN[l, dn] * (q + qs) + ON[kind, dn] * (p - ps)
        low, high = vertical(q, at)
        change = vertical_mix * ((low - q) + (high - q)) - ((te - roll(te, 1)) + (tn - ts))
        if heat is not None:
            change = change + heat
        return q + F[MASK, levels if kind == 1 else 0, at] * change

    def advance(B, C, t, packing):
        first_pass(B, levels, 1)
        for r in range(BASE, end, CHUNK):
            own = slice(r - BASE, r - BASE + CHUNK)

            def beside(q, at):
                return (
                    jnp.where(first_c, q, roll(q, 16)),
                    jnp.where(last_c, q, roll(q, -16)),
                )

            res = second_pass(B, levels, 1, r, beside, FE[own] if t == 0 else None)
            R2[own] = jnp.where(jc_low, roll(res, -10), roll(res, -2))

        def level(l, carry):
            first_pass(B, l, 0)
            back = lax.rem(2 * LANES - 2 - 16 * l, LANES)
            ahead = lax.rem(16 * l + 8, LANES)
            lower, upper = jnp.maximum(l - 1, 0), jnp.minimum(l + 1, levels - 1)
            gain = jnp.where(l == 0, heat_gain, 0.0).astype(jnp.float32)
            for r in range(BASE, end, CHUNK):
                own = slice(r - BASE, r - BASE + CHUNK)
                res = second_pass(
                    B, l, 0, r, lambda q, at: (B[lower, at], B[upper, at]), gain * FL[own] if t == 0 else None
                )
                res = jnp.where(rim_c, roll(R2[own], back), res)
                C[l, r : r + CHUNK] = res
                if packing:
                    A[own] = jnp.where(group_c == l, roll(res, ahead), A[own])
            if not packing:
                pltpu.make_async_copy(C.at[l, BASE:end], out.at[t, l], out_sem.at[t, l]).start()
            return carry

        lax.fori_loop(0, levels, level, 0)

    later = ((1, 5, 6, 5, 6), (2, 6, 7, 6, 7))
    for t in (0, 1):
        advance(F.at[1 + t], G.at[t], t, True)
        finish_pack(G.at[t], 5 + t, lambda i: A[8 * i : 8 * i + 8])
        send_ew(*later[t])
        pack_rows(G.at[t], 5 + t)
        send_ns(*later[t])
    for t in (0, 1):
        wait_all(*later[t])
        unpack_rows(G.at[t], 5 + t)
        unpack_cols(G.at[t], 5 + t)
        advance(G.at[t], F.at[1 + t], t, False)

    pl.when(jnp.logical_not(top))(atm_up.wait_send)
    pl.when(inner)(atm_down.wait_send)
    wait_sent(*first)
    for t in (0, 1):
        wait_sent(*later[t])
    flux_copy.wait()

    def finish(l, carry):
        for t in (0, 1):
            pltpu.make_async_copy(F.at[1 + t, l, BASE:end], out.at[t, l], out_sem.at[t, l]).wait()
        return carry

    lax.fori_loop(0, levels, finish, 0)


def solution(mesh):
    lat_n, lon_n = mesh.shape["lat"], mesh.shape["lon"]

    def per_device(tracers, velocities, land_mask, atm_flux, atm_id, intersection_count, weight_tiles):
        _, levels, rows, cols = tracers.shape
        blocks, entries, block_rows, _ = weight_tiles.shape
        local_atm = atm_flux.shape[0] // block_rows
        planes = levels + 1
        tall = rows + 2 * BASE
        fold_rows = rows // 8
        f32 = jnp.float32
        hbm = pl.BlockSpec(memory_space=pltpu.HBM)
        smem = pl.BlockSpec(memory_space=pltpu.SMEM)
        return pl.pallas_call(
            functools.partial(kernel, lat_n, lon_n, levels, rows, blocks, entries, block_rows, local_atm),
            out_shape=(
                jax.ShapeDtypeStruct(tracers.shape, f32),
                jax.ShapeDtypeStruct((rows, cols), f32),
            ),
            in_specs=[hbm, hbm, hbm, hbm, hbm, smem, smem],
            out_specs=(hbm, hbm),
            scratch_shapes=[
                pltpu.VMEM((5, planes, tall, cols), f32),
                pltpu.VMEM((2, planes, tall, cols), f32),
                pltpu.VMEM((rows, cols), jnp.int32),
                pltpu.VMEM((planes, tall, cols), f32),
                pltpu.VMEM((planes, tall, cols), f32),
                pltpu.VMEM((2, tall, cols), f32),
                pltpu.VMEM((2, tall, cols), f32),
                pltpu.VMEM((tall, cols), f32),
                pltpu.VMEM((rows, cols), f32),
                pltpu.VMEM((rows, cols), f32),
                pltpu.VMEM((rows, cols), f32),
                pltpu.VMEM((rows, cols), f32),
                pltpu.VMEM(((local_atm + 4) * block_rows, cols), f32),
                pltpu.VMEM(weight_tiles.shape, f32),
                pltpu.VMEM((rows, (local_atm + 4) * block_rows), f32),
                pltpu.VMEM((2, 7, 24, cols), f32),
                pltpu.VMEM((2, 7, 24, cols), f32),
                pltpu.VMEM((4, 7, 8, cols), f32),
                pltpu.VMEM((2, 7, fold_rows, cols), f32),
                pltpu.VMEM((2, 7, fold_rows, cols), f32),
                pltpu.SemaphoreType.DMA((8,)),
                pltpu.SemaphoreType.DMA((2, levels)),
                pltpu.SemaphoreType.DMA((3, 8)),
                pltpu.SemaphoreType.DMA((3, 8)),
                pltpu.SemaphoreType.DMA((4,)),
            ],
            compiler_params=pltpu.CompilerParams(
                collective_id=0, has_side_effects=True, vmem_limit_bytes=62 * 1024 * 1024
            ),
        )(tracers, velocities, land_mask, atm_flux, weight_tiles, atm_id.T, intersection_count)

    in_specs = (
        P(None, "ens", "lat", "lon"),
        P(None, "ens", "lat", "lon"),
        P("lat", "lon"),
        P(("ens", "lat"), "lon"),
        P("lat", None),
        P("lat"),
        P("lat", None, None, None),
    )
    out_specs = (P(None, "ens", "lat", "lon"), P(("ens", "lat"), "lon"))
    return jax.shard_map(
        per_device, mesh=mesh, in_specs=in_specs, out_specs=out_specs, check_vma=False
    )
```

```python
import functools

import jax
import jax.numpy as jnp
from jax import lax
from jax.experimental import pallas as pl
from jax.experimental.pallas import tpu as pltpu
from jax.sharding import PartitionSpec as P

lateral_mix = 0.06
biharmonic_mix = 0.015
vertical_mix = 0.15
heat_gain = 0.5

LANES = 128
BASE = 16
CHUNK = 32
MESH = pl.DeviceIdType.MESH
V, MASK, U = 0, 3, 4


def roll(x, shift):
    return pltpu.roll(x, shift % LANES if isinstance(shift, int) else shift, x.ndim - 1)


def kernel(
    lat_n, lon_n, levels, rows, blocks, entries, block_rows, local_atm,
    tr, vel, mask_in, atm, wt, ids, cnt, out, flux_out,
    F, G, MI, HE, HN, OE, ON, PL, A, R2, FE, FL, ATM, WT, WB,
    SNS, RNS, RC, SEW, REW,
    in_sem, out_sem, send_sem, recv_sem, atm_sem,
):
    end = BASE + rows
    tiles = rows // 8
    third = tiles // 8
    fold_rows = third * 8
    lat, lon = lax.axis_index("lat"), lax.axis_index("lon")
    top = lat == lat_n - 1
    bottom = lat == 0
    west = lax.rem(lon + lon_n - 1, lon_n)
    east = lax.rem(lon + 1, lon_n)
    up_lat = jnp.where(top, lat, lat + 1)
    up_lon = jnp.where(top, lon_n - 1 - lon, lon)
    a_lon = jnp.where(top, lax.rem(lon_n - lon, lon_n), east)
    b_lon = jnp.where(top, lax.rem(2 * lon_n - 2 - lon, lon_n), west)
    a_self = jnp.logical_and(top, a_lon == lon)
    b_self = jnp.logical_and(top, b_lon == lon)
    a_away = jnp.logical_not(a_self)
    b_away = jnp.logical_not(b_self)
    inner = jnp.logical_not(bottom)
    below = jnp.maximum(lat - 1, 0)
    up_slot = jnp.where(top, 0, 1)
    a_slot = jnp.where(top, 0, 2)
    b_slot = jnp.where(top, 1, 3)

    lane = lax.broadcasted_iota(jnp.int32, (8, LANES), 1)
    lane_c = lax.broadcasted_iota(jnp.int32, (CHUNK, LANES), 1)
    j8 = lane & 15
    group8 = lane >> 4
    pair8 = j8 >> 1
    low8, high8, half8 = j8 < 4, j8 >= 12, j8 < 8
    group_c = lane_c >> 4
    jc_low = (lane_c & 15) < 2
    rim_c = (lane_c < 2) | (lane_c >= LANES - 2)
    first_c, last_c = lane_c < 16, lane_c >= LANES - 16

    loads = [
        pltpu.make_async_copy(vel.at[1], F.at[V, 0:levels, BASE:end], in_sem.at[0]),
        pltpu.make_async_copy(tr.at[0], F.at[1, 0:levels, BASE:end], in_sem.at[1]),
        pltpu.make_async_copy(tr.at[1], F.at[2, 0:levels, BASE:end], in_sem.at[2]),
        pltpu.make_async_copy(mask_in, MI, in_sem.at[3]),
        pltpu.make_async_copy(vel.at[0], F.at[U, 0:levels, BASE:end], in_sem.at[4]),
        pltpu.make_async_copy(atm, ATM.at[2 * block_rows : 2 * block_rows + local_atm * block_rows], in_sem.at[5]),
        pltpu.make_async_copy(wt, WT, in_sem.at[6]),
    ]
    for copy in (loads[5], loads[3], loads[1], loads[2], loads[4], loads[0], loads[6]):
        copy.start()

    barrier = pltpu.get_barrier_semaphore()

    def greet(lat_to, lon_to):
        pl.semaphore_signal(barrier, inc=1, device_id={"lat": lat_to, "lon": lon_to}, device_id_type=MESH)

    greet(lat, west)
    greet(lat, east)
    greet(up_lat, up_lon)
    pl.when(a_away)(lambda: greet(up_lat, a_lon))
    pl.when(b_away)(lambda: greet(up_lat, b_lon))

    @pl.when(inner)
    def _():
        greet(below, lon)
        greet(below, west)
        greet(below, east)

    zero8 = jnp.zeros((8, LANES), jnp.float32)

    def zero_slot(s, carry):
        for side in (0, 1):
            SNS[side, s, 16:24] = zero8
        return carry

    lax.fori_loop(0, 7, zero_slot, 0)

    @pl.when(bottom)
    def _():
        def clear(s, carry):
            for tile in range(3):
                RNS[1, s, 8 * tile : 8 * tile + 8] = zero8
            RC[2, s] = zero8
            RC[3, s] = zero8
            return carry

        lax.fori_loop(0, 7, clear, 0)
        for tile in range(2 * block_rows // 8):
            ATM[8 * tile : 8 * tile + 8] = zero8

    atm_end = (2 + local_atm) * block_rows

    @pl.when(top)
    def _():
        for tile in range(2 * block_rows // 8):
            ATM[atm_end + 8 * tile : atm_end + 8 * tile + 8] = zero8

    def remote(src, dst, send, recv, lat_to, lon_to):
        return pltpu.make_async_remote_copy(
            src_ref=src, dst_ref=dst, send_sem=send, recv_sem=recv,
            device_id={"lat": lat_to, "lon": lon_to}, device_id_type=MESH,
        )

    def messages(ph, n0, n1, e0, e1):
        s, r = send_sem, recv_sem
        edge = lambda side: SNS.at[side, n0:n1, 16:24]
        return {
            "up": remote(SNS.at[0, n0:n1], RNS.at[up_slot, n0:n1], s.at[ph, 0], r.at[ph, up_slot], up_lat, up_lon),
            "a": remote(edge(0), RC.at[a_slot, n0:n1], s.at[ph, 2], r.at[ph, 2 + a_slot], up_lat, a_lon),
            "b": remote(edge(0), RC.at[b_slot, n0:n1], s.at[ph, 3], r.at[ph, 2 + b_slot], up_lat, b_lon),
            "down": remote(SNS.at[1, n0:n1], RNS.at[0, n0:n1], s.at[ph, 1], r.at[ph, 0], below, lon),
            "se": remote(edge(1), RC.at[0, n0:n1], s.at[ph, 4], r.at[ph, 2], below, east),
            "sw": remote(edge(1), RC.at[1, n0:n1], s.at[ph, 5], r.at[ph, 3], below, west),
            "w": remote(SEW.at[0, e0:e1], REW.at[1, e0:e1], s.at[ph, 6], r.at[ph, 7], lat, west),
            "e": remote(SEW.at[1, e0:e1], REW.at[0, e0:e1], s.at[ph, 7], r.at[ph, 6], lat, east),
        }

    def arrivals(ph, n0, n1, e0, e1):
        s, r = send_sem, recv_sem
        edge = SNS.at[0, n0:n1, 16:24]
        got = {}
        for slot in (0, 1):
            got[slot] = remote(SNS.at[0, n0:n1], RNS.at[slot, n0:n1], s.at[ph, 0], r.at[ph, slot], lat, west)
        for slot in range(4):
            got[2 + slot] = remote(edge, RC.at[slot, n0:n1], s.at[ph, 2], r.at[ph, 2 + slot], lat, west)
        for slot in (0, 1):
            got[6 + slot] = remote(SEW.at[0, e0:e1], REW.at[slot, e0:e1], s.at[ph, 6], r.at[ph, 6 + slot], lat, west)
        return got

    def send_ew(ph, n0, n1, e0, e1):
        m = messages(ph, n0, n1, e0, e1)
        m["w"].start()
        m["e"].start()

    def send_ns(ph, n0, n1, e0, e1):
        m = messages(ph, n0, n1, e0, e1)

        @pl.when(inner)
        def _():
            m["down"].start()
            m["se"].start()
            m["sw"].start()

        @pl.when(top)
        def _():
            r_i = lax.broadcasted_iota(jnp.int32, (LANES, LANES), 0)
            c_i = lax.broadcasted_iota(jnp.int32, (LANES, LANES), 1)
            whole = jnp.where(r_i + c_i == LANES - 1, 1.0, 0.0).astype(jnp.float32)
            group = jnp.where((r_i // 16 == c_i // 16) & (r_i % 16 + c_i % 16 == 15), 1.0, 0.0).astype(jnp.float32)
            count = n1 - n0
            body = jnp.concatenate([SNS[0, f, 0:16] for f in range(n0, n1)], 0)
            tail = jnp.concatenate([SNS[0, f, 16:24] for f in range(n0, n1)], 0)
            body = jnp.dot(body, whole, precision=lax.Precision.HIGHEST, preferred_element_type=jnp.float32)
            tail = jnp.dot(tail, group, precision=lax.Precision.HIGHEST, preferred_element_type=jnp.float32)
            for i in range(count):
                sign = -1.0 if n0 + i == V else 1.0
                SNS[0, n0 + i, 0:16] = sign * body[16 * i : 16 * i + 16]
                SNS[0, n0 + i, 16:24] = sign * tail[8 * i : 8 * i + 8]

        m["up"].start()
        pl.when(a_away)(m["a"].start)
        pl.when(b_away)(m["b"].start)

        @pl.when(a_self)
        def _():
            for f in range(n0, n1):
                RC[0, f] = SNS[0, f, 16:24]

        @pl.when(b_self)
        def _():
            for f in range(n0, n1):
                RC[1, f] = SNS[0, f, 16:24]

    def wait_all(ph, n0, n1, e0, e1):
        got = arrivals(ph, n0, n1, e0, e1)
        got[0].wait_recv()
        pl.when(a_away)(got[2].wait_recv)
        pl.when(b_away)(got[3].wait_recv)
        got[6].wait_recv()
        got[7].wait_recv()

        @pl.when(inner)
        def _():
            got[1].wait_recv()
            got[4].wait_recv()
            got[5].wait_recv()

    def wait_sent(ph, n0, n1, e0, e1):
        m = messages(ph, n0, n1, e0, e1)
        m["up"].wait_send()
        m["w"].wait_send()
        m["e"].wait_send()
        pl.when(a_away)(m["a"].wait_send)
        pl.when(b_away)(m["b"].wait_send)

        @pl.when(inner)
        def _():
            m["down"].wait_send()
            m["se"].wait_send()
            m["sw"].wait_send()

    def finish_pack(B, s, gather):
        to_w = [zero8] * third
        to_e = [zero8] * third
        gathered = [gather(i) for i in range(tiles)]
        owns = [jnp.where(half8, roll(a, -4), roll(a, 4)) for a in gathered]
        for i, own in enumerate(owns):
            B[levels, BASE + 8 * i : BASE + 8 * i + 8] = own
            p, r = i // third, i % third
            here = pair8 == p
            to_w[r] = jnp.where(here, roll(own, 2 * p - 4), to_w[r])
            to_e[r] = jnp.where(here, roll(own, 2 * p - 10), to_e[r])
        for r in range(third):
            SEW[0, s, 8 * r : 8 * r + 8] = to_w[r]
            SEW[1, s, 8 * r : 8 * r + 8] = to_e[r]

    def pack_rows(B, s):
        for side, first, second in ((0, end - 1, end - 2), (1, BASE, BASE + 1)):
            for l in range(levels):
                SNS[side, s, l : l + 1] = B[l, first : first + 1]
                SNS[side, s, levels + l : levels + l + 1] = B[l, second : second + 1]
            SNS[side, s, 16:17] = B[levels, first : first + 1]
            SNS[side, s, 17:18] = B[levels, second : second + 1]

    def gather_planes(B):
        def gather(i):
            a = zero8
            for l in range(levels):
                a = jnp.where(group8 == l, roll(B[l, BASE + 8 * i : BASE + 8 * i + 8], 16 * l + 8), a)
            return a

        return gather

    def unpack_rows(B, s):
        for l in range(levels):
            B[l, end : end + 1] = RNS[0, s, l : l + 1]
            B[l, end + 1 : end + 2] = RNS[0, s, levels + l : levels + l + 1]
            B[l, BASE - 1 : BASE] = RNS[1, s, l : l + 1]
            B[l, BASE - 2 : BASE - 1] = RNS[1, s, levels + l : levels + l + 1]
        for side, first, second in ((0, end, end + 1), (1, BASE - 1, BASE - 2)):
            own = RNS[side, s, 16:24]
            w = roll(RC[2 * side, s], -8)
            e = roll(RC[2 * side + 1, s], 8)
            x = jnp.where(low8, w, jnp.where(high8, e, own))
            B[levels, first : first + 1] = x[0:1]
            B[levels, second : second + 1] = x[1:2]

    def unpack_cols(B, s):
        for i in range(tiles):
            p, r = i // third, i % third
            at = slice(BASE + 8 * i, BASE + 8 * i + 8)
            w = roll(REW[0, s, 8 * r : 8 * r + 8], 2 - 2 * p)
            e = roll(REW[1, s, 8 * r : 8 * r + 8], 12 - 2 * p)
            B[levels, at] = jnp.where(low8, w, jnp.where(high8, e, B[levels, at]))

    loads[3].wait()

    def spread_mask(l, carry):
        F[MASK, l, BASE:end] = MI[...].astype(jnp.float32)
        return carry

    lax.fori_loop(0, levels, spread_mask, 0)
    def pack_field(f, carry):
        B = F.at[f]
        finish_pack(B, f, gather_planes(B))
        pack_rows(B, f)
        return carry

    for f in (MASK, 1, 2, U, V):
        if f != MASK:
            loads[f].wait()
        pack_field(f, 0)

    pl.semaphore_wait(
        barrier, 3 + jnp.where(a_away, 1, 0) + jnp.where(b_away, 1, 0) + jnp.where(inner, 3, 0)
    )
    reach = 2 * block_rows
    loads[5].wait()
    atm_up = remote(ATM.at[atm_end - reach : atm_end], ATM.at[0:reach], atm_sem.at[0], atm_sem.at[2], up_lat, up_lon)
    atm_down = remote(
        ATM.at[reach : 2 * reach], ATM.at[atm_end : atm_end + reach], atm_sem.at[1], atm_sem.at[3], below, lon
    )
    pl.when(jnp.logical_not(top))(atm_up.start)
    pl.when(inner)(atm_down.start)

    first = (0, 0, 4, 1, 5)
    send_ew(*first)
    send_ns(*first)

    loads[6].wait()
    slots = local_atm + 4
    wide = slots * block_rows
    spread = jnp.where(
        lax.broadcasted_iota(jnp.int32, (block_rows, wide), 1) % block_rows
        == lax.broadcasted_iota(jnp.int32, (block_rows, wide), 0),
        1.0, 0.0,
    ).astype(jnp.float32)
    slot_of = lax.broadcasted_iota(jnp.int32, (block_rows, wide), 1) // block_rows

    def build(b, carry):
        flat = jnp.concatenate([WT[b, k] for k in range(entries)], 0)
        copies = jnp.dot(flat, spread, precision=lax.Precision.HIGHEST, preferred_element_type=jnp.float32)
        total = jnp.zeros((block_rows, wide), jnp.float32)
        for k in range(entries):
            slot = jnp.where(k < cnt[b], ids[k, b] - lat * local_atm + 2, -1)
            total = total + jnp.where(slot_of == slot, copies[k * block_rows : (k + 1) * block_rows], 0.0)
        WB[pl.ds(pl.multiple_of(b * block_rows, block_rows), block_rows)] = total
        return carry

    lax.fori_loop(0, blocks, build, 0)
    pl.when(inner)(
        remote(ATM.at[0:reach], ATM.at[0:reach], atm_sem.at[0], atm_sem.at[2], lat, west).wait_recv
    )
    pl.when(jnp.logical_not(top))(
        remote(ATM.at[0:reach], ATM.at[atm_end : atm_end + reach], atm_sem.at[1], atm_sem.at[3], lat, west).wait_recv
    )
    FL[...] = jnp.dot(WB[...], ATM[...], precision=lax.Precision.HIGHEST, preferred_element_type=jnp.float32)
    flux_copy = pltpu.make_async_copy(FL, flux_out, in_sem.at[7])
    flux_copy.start()
    for i in range(tiles):
        at = slice(8 * i, 8 * i + 8)
        a = roll(FL[at], 8)
        own = jnp.where(half8, roll(a, -4), roll(a, 4))
        FE[at] = jnp.where(lane < 16, heat_gain * own, 0.0)

    def mask_tables(kind, plane, starts):
        for r in starts:
            m = F[MASK, plane, r : r + 8]
            OE[kind, r : r + 8] = m * roll(m, -1)
            ON[kind, r : r + 8] = m * F[MASK, plane, r + 1 : r + 9]

    def face_tables(l, kind, starts):
        for r in starts:
            at = slice(r, r + 8)
            HN[l, at] = 0.25 * ON[kind, at] * (F[V, l, at] + F[V, l, r + 1 : r + 9])
            if r >= BASE:
                u = F[U, l, at]
                HE[l, at] = 0.25 * OE[kind, at] * (u + roll(u, -1))

    mask_tables(0, 0, range(BASE, end - 8, 8))

    def own_tables(l, carry):
        face_tables(l, 0, range(BASE, end - 8, 8))
        return carry

    lax.fori_loop(0, levels, own_tables, 0)

    wait_all(*first)

    def place_rows(f, carry):
        unpack_rows(F.at[f], f)
        return carry

    def place_cols(f, carry):
        unpack_cols(F.at[f], f)
        return carry

    lax.fori_loop(0, 4, place_rows, 0)
    lax.fori_loop(1, 5, place_cols, 0)

    mask_tables(0, 0, (8, end - 8, end))
    mask_tables(1, levels, range(8, end + 8, 8))

    def rim_tables(l, carry):
        face_tables(l, 0, (8, end - 8))
        return carry

    lax.fori_loop(0, levels, rim_tables, 0)
    face_tables(levels, 1, range(8, end, 8))

    def first_pass(B, l, kind):
        for r in range(8, end + 8, 16):
            at = slice(r, r + 16)
            q = B[l, at]
            ge = OE[kind, at] * (roll(q, -1) - q)
            lap = (ge - roll(ge, 1)) + (
                ON[kind, at] * (B[l, r + 1 : r + 17] - q)
                - ON[kind, r - 1 : r + 15] * (q - B[l, r - 1 : r + 15])
            )
            PL[at] = biharmonic_mix * lap - lateral_mix * q

    def second_pass(B, l, kind, r, vertical, heat):
        at, up, dn = slice(r, r + CHUNK), slice(r + 1, r + 1 + CHUNK), slice(r - 1, r - 1 + CHUNK)
        q, qn, qs = B[l, at], B[l, up], B[l, dn]
        p, pn, ps = PL[at], PL[up], PL[dn]
        te = HE[l, at] * (q + roll(q, -1)) + OE[kind, at] * (roll(p, -1) - p)
        tn = HN[l, at] * (q + qn) + ON[kind, at] * (pn - p)
        ts = HN[l, dn] * (q + qs) + ON[kind, dn] * (p - ps)
        low, high = vertical(q, at)
        change = vertical_mix * ((low - q) + (high - q)) - ((te - roll(te, 1)) + (tn - ts))
        if heat is not None:
            change = change + heat
        return q + F[MASK, levels if kind == 1 else 0, at] * change

    def advance(B, C, t, packing):
        first_pass(B, levels, 1)
        for r in range(BASE, end, CHUNK):
            own = slice(r - BASE, r - BASE + CHUNK)

            def beside(q, at):
                return (
                    jnp.where(first_c, q, roll(q, 16)),
                    jnp.where(last_c, q, roll(q, -16)),
                )

            res = second_pass(B, levels, 1, r, beside, FE[own] if t == 0 else None)
            R2[own] = jnp.where(jc_low, roll(res, -10), roll(res, -2))

        def level(l, carry):
            first_pass(B, l, 0)
            back = lax.rem(2 * LANES - 2 - 16 * l, LANES)
            ahead = lax.rem(16 * l + 8, LANES)
            lower, upper = jnp.maximum(l - 1, 0), jnp.minimum(l + 1, levels - 1)
            gain = jnp.where(l == 0, heat_gain, 0.0).astype(jnp.float32)
            for r in range(BASE, end, CHUNK):
                own = slice(r - BASE, r - BASE + CHUNK)
                res = second_pass(
                    B, l, 0, r, lambda q, at: (B[lower, at], B[upper, at]), gain * FL[own] if t == 0 else None
                )
                res = jnp.where(rim_c, roll(R2[own], back), res)
                C[l, r : r + CHUNK] = res
                if packing:
                    A[own] = jnp.where(group_c == l, roll(res, ahead), A[own])
            if not packing:
                pltpu.make_async_copy(C.at[l, BASE:end], out.at[t, l], out_sem.at[t, l]).start()
            return carry

        lax.fori_loop(0, levels, level, 0)

    later = ((1, 5, 6, 5, 6), (2, 6, 7, 6, 7))
    for t in (0, 1):
        advance(F.at[1 + t], G.at[t], t, True)
        finish_pack(G.at[t], 5 + t, lambda i: A[8 * i : 8 * i + 8])
        send_ew(*later[t])
        pack_rows(G.at[t], 5 + t)
        send_ns(*later[t])
    for t in (0, 1):
        wait_all(*later[t])
        unpack_rows(G.at[t], 5 + t)
        unpack_cols(G.at[t], 5 + t)
        advance(G.at[t], F.at[1 + t], t, False)

    pl.when(jnp.logical_not(top))(atm_up.wait_send)
    pl.when(inner)(atm_down.wait_send)
    wait_sent(*first)
    for t in (0, 1):
        wait_sent(*later[t])
    flux_copy.wait()

    def finish(l, carry):
        for t in (0, 1):
            pltpu.make_async_copy(F.at[1 + t, l, BASE:end], out.at[t, l], out_sem.at[t, l]).wait()
        return carry

    lax.fori_loop(0, levels, finish, 0)


def solution(mesh):
    lat_n, lon_n = mesh.shape["lat"], mesh.shape["lon"]

    def per_device(tracers, velocities, land_mask, atm_flux, atm_id, intersection_count, weight_tiles):
        _, levels, rows, cols = tracers.shape
        blocks, entries, block_rows, _ = weight_tiles.shape
        local_atm = atm_flux.shape[0] // block_rows
        planes = levels + 1
        tall = rows + 2 * BASE
        fold_rows = rows // 8
        f32 = jnp.float32
        hbm = pl.BlockSpec(memory_space=pltpu.HBM)
        smem = pl.BlockSpec(memory_space=pltpu.SMEM)
        return pl.pallas_call(
            functools.partial(kernel, lat_n, lon_n, levels, rows, blocks, entries, block_rows, local_atm),
            out_shape=(
                jax.ShapeDtypeStruct(tracers.shape, f32),
                jax.ShapeDtypeStruct((rows, cols), f32),
            ),
            in_specs=[hbm, hbm, hbm, hbm, hbm, smem, smem],
            out_specs=(hbm, hbm),
            scratch_shapes=[
                pltpu.VMEM((5, planes, tall, cols), f32),
                pltpu.VMEM((2, planes, tall, cols), f32),
                pltpu.VMEM((rows, cols), jnp.int32),
                pltpu.VMEM((planes, tall, cols), f32),
                pltpu.VMEM((planes, tall, cols), f32),
                pltpu.VMEM((2, tall, cols), f32),
                pltpu.VMEM((2, tall, cols), f32),
                pltpu.VMEM((tall, cols), f32),
                pltpu.VMEM((rows, cols), f32),
                pltpu.VMEM((rows, cols), f32),
                pltpu.VMEM((rows, cols), f32),
                pltpu.VMEM((rows, cols), f32),
                pltpu.VMEM(((local_atm + 4) * block_rows, cols), f32),
                pltpu.VMEM(weight_tiles.shape, f32),
                pltpu.VMEM((rows, (local_atm + 4) * block_rows), f32),
                pltpu.VMEM((2, 7, 24, cols), f32),
                pltpu.VMEM((2, 7, 24, cols), f32),
                pltpu.VMEM((4, 7, 8, cols), f32),
                pltpu.VMEM((2, 7, fold_rows, cols), f32),
                pltpu.VMEM((2, 7, fold_rows, cols), f32),
                pltpu.SemaphoreType.DMA((8,)),
                pltpu.SemaphoreType.DMA((2, levels)),
                pltpu.SemaphoreType.DMA((3, 8)),
                pltpu.SemaphoreType.DMA((3, 8)),
                pltpu.SemaphoreType.DMA((4,)),
            ],
            compiler_params=pltpu.CompilerParams(
                collective_id=0, has_side_effects=True, vmem_limit_bytes=62 * 1024 * 1024
            ),
        )(tracers, velocities, land_mask, atm_flux, weight_tiles, atm_id.T, intersection_count)

    in_specs = (
        P(None, "ens", "lat", "lon"),
        P(None, "ens", "lat", "lon"),
        P("lat", "lon"),
        P(("ens", "lat"), "lon"),
        P("lat", None),
        P("lat"),
        P("lat", None, None, None),
    )
    out_specs = (P(None, "ens", "lat", "lon"), P(("ens", "lat"), "lon"))
    return jax.shard_map(
        per_device, mesh=mesh, in_specs=in_specs, out_specs=out_specs, check_vma=False
    )
```
